256 devices in a mesh: region: 8 (over y, x_hi), view: 32 (over z, x_lo, core).
Axes of the slice: x: 4 (x_hi: 2, x_lo: 2; x = x_hi * 2 + x_lo), y: 4, z: 8, core: 2. Of those that a mesh axis runs over, the one named last changes fastest.
Arguments:
- hidden: bfloat16 [32768, 1152], P(('region', 'view')), may hold values from -12 to 12, as said below
- pairs: int32 [1024, 2], replicated, may hold values from -1 to 255, as said below
- w_query: bfloat16 [1152, 1152], replicated, may hold values from -0.1875 to 0.1875
- w_key: bfloat16 [1152, 1152], replicated, may hold values from -0.1875 to 0.1875
- w_value: bfloat16 [1152, 1152], replicated, may hold values from -0.1875 to 0.1875
- w_out: bfloat16 [1152, 1152], replicated, may hold values from -0.1875 to 0.1875
Outputs:
- attended: bfloat16 [32768, 1152], P(('region', 'view'))
The draws below stay inside these ranges and needn't reach their ends.
Inputs may be any that keep to these rules, and one draw needn't show every extreme that they name: hidden is of order one per entry. `pairs`: A row is either (-1, -1), which lists nothing, or (g, g2) with g < g2: either g2 = g + 32 in the next region with the same place in it, or g2 lies in g's region and its place minus g's place, taken modulo 32, is 1, 6 or 32 // 2 (or the same with g and g2 exchanged). Every view is linked with the view of its region whose place differs by 16. No pair is listed twice, and no view is linked to more than 8 others.
All inputs are finite; a program needn't handle non-finite values.
Results may differ from the reference program's by a relative error of at most 0.012.
The reference program's roundings to bfloat16 on the way (of `rounded` and `mixed`) count: a program that leaves them out, or rounds other values in their place, can miss the bound.
Values may be sent and summed in bfloat16 or wider, within the bound.
A program may use at most 192 MiB of HBM per device.

```python
import jax
import jax.numpy as jnp
from jax import lax

D = 1152
HEADS = 16
HEAD_SIZE = 72
TOK = 128
LINK_SLOTS = 4
MAX_LINKS = 9
REGION_VIEWS = 32
REGIONS = 8
VIEWS = 256


def draw_hidden(key, part):
    key = jax.random.fold_in(key, 7)
    first = jax.random.fold_in(key, 0)
    base = jnp.clip(jax.random.normal(first, (VIEWS * TOK, D), jnp.float32), -6.0, 6.0)
    return base.astype(jnp.bfloat16)


def draw_pairs(key, part):
    key = jax.random.fold_in(key, 11)
    first, third = jax.random.split(key)
    ids = jnp.arange(VIEWS, dtype=jnp.int32)
    region = ids // REGION_VIEWS
    place = ids % REGION_VIEWS
    spacing = max(REGION_VIEWS // 6, 1)
    half_way = REGION_VIEWS // 2
    level = jax.random.randint(first, (VIEWS,), 1, 5)
    offset_row = jnp.array([1, 1 + spacing, half_way], jnp.int32)
    offsets = offset_row[None, :] + jnp.zeros((VIEWS, 3), jnp.int32)
    inside = region[:, None] * REGION_VIEWS + (place[:, None] + offsets) % REGION_VIEWS
    partner = jnp.concatenate([inside, (ids + REGION_VIEWS)[:, None]], axis=1)
    throws = jax.random.randint(third, (VIEWS, LINK_SLOTS), 0, 4)
    allowed = jnp.stack([jnp.ones((VIEWS,), bool), jnp.ones((VIEWS,), bool), place < half_way, region < REGIONS - 1], axis=1)
    forced = jnp.arange(LINK_SLOTS, dtype=jnp.int32)[None, :] == 2
    keep = ((throws < level[:, None]) | forced) & allowed
    lower = jnp.minimum(ids[:, None], partner)
    upper = jnp.maximum(ids[:, None], partner)
    first_col = jnp.where(keep, lower, -1).reshape(-1)
    second_col = jnp.where(keep, upper, -1).reshape(-1)
    return jnp.stack([first_col, second_col], axis=1).astype(jnp.int32)


def bell_draw(key, shape, spread, most, kind=jnp.bfloat16):
    return jnp.clip(spread * jax.random.normal(key, shape, jnp.float32), -most, most).astype(kind)


def setup_inputs(seed: int = 0) -> dict:
    streams_of = jax.random.split(jax.random.key(seed), 7)
    hidden = draw_hidden(jax.random.fold_in(streams_of[6], 71), 0)
    pairs = draw_pairs(jax.random.fold_in(streams_of[6], 71), 0)
    w_query = bell_draw(streams_of[2], (D, D), D ** -0.5, 0.1875)
    w_key = bell_draw(streams_of[3], (D, D), D ** -0.5, 0.1875)
    w_value = bell_draw(streams_of[4], (D, D), D ** -0.5, 0.1875)
    w_out = bell_draw(streams_of[5], (D, D), D ** -0.5, 0.1875)
    return dict(hidden=hidden, pairs=pairs, w_query=w_query, w_key=w_key, w_value=w_value, w_out=w_out)


def reference(hidden, pairs, w_query, w_key, w_value, w_out):
    def project(weight):
        return jnp.dot(hidden, weight, preferred_element_type=jnp.float32).astype(jnp.bfloat16)

    query = project(w_query).reshape(VIEWS, TOK, HEADS, HEAD_SIZE)
    keys = project(w_key).reshape(VIEWS, TOK, HEADS, HEAD_SIZE)
    values = project(w_value).reshape(VIEWS, TOK, HEADS, HEAD_SIZE)
    ids = jnp.arange(VIEWS, dtype=jnp.int32)
    left = (pairs[:, 0][:, None] == ids[None, :]).astype(jnp.float32)
    right = (pairs[:, 1][:, None] == ids[None, :]).astype(jnp.float32)
    links = jnp.dot(left.T, right, precision=lax.Precision.HIGHEST)
    linked = ((links + links.T) > 0.5) | (ids[:, None] == ids[None, :])

    def per_view(view):
        row = linked[view]
        count = jnp.sum(row.astype(jnp.int32))
        picks = jnp.nonzero(row, size=MAX_LINKS, fill_value=view)[0].astype(jnp.int32)
        valid = jnp.arange(MAX_LINKS, dtype=jnp.int32) < count
        own = query[view].astype(jnp.float32)
        near_keys = keys[picks].astype(jnp.float32)
        near_values = values[picks].astype(jnp.float32)
        scores = jnp.einsum("qhe,jkhe->hqjk", own, near_keys) * (HEAD_SIZE ** -0.5)
        scores = jnp.where(valid[None, None, :, None], scores, -1e30)
        top = jnp.max(scores, axis=(2, 3), keepdims=True)
        weights = jnp.exp(scores - top)
        totals = jnp.sum(weights, axis=(2, 3))
        rounded = lax.optimization_barrier(weights.astype(jnp.bfloat16)).astype(jnp.float32)
        summed = jnp.einsum("hqjk,jkhe->qhe", rounded, near_values)
        mixed = summed / totals.T[:, :, None]
        return mixed.reshape(TOK, D).astype(jnp.bfloat16)

    mixed = lax.map(per_view, ids).reshape(VIEWS * TOK, D)
    return jnp.dot(mixed, w_out, preferred_element_type=jnp.float32).astype(jnp.bfloat16)
```

```python
import functools

import jax
import jax.numpy as jnp
import numpy as np
from jax import lax
from jax.experimental import pallas as pl
from jax.experimental.pallas import tpu as pltpu
from jax.sharding import PartitionSpec as P

MESH = pl.DeviceIdType.MESH
BF, F32 = jnp.bfloat16, jnp.float32
D, TOK, HEADS, HEAD = 1152, 128, 16, 72
NEG = -1e30
SCALE2 = float(HEAD**-0.5 * np.log2(np.e))
NT = (((1,), (1,)), ((), ()))

WINDOWS = ((0, (0, 1, 2)), (1, (3, 4)), (2, (5, 6)), (3, (7,)), (4, (8, 9)), (5, (10, 11)), (6, (12, 13)), (7, (14, 15)))

OWN, SIB, STEP1, REG1, REG2, NEAR6, FAR6, HALF = range(8)

CHUNKS = ((0, 640, "a"), (640, 512, "b"))
GROUPS = ((OWN, SIB), (STEP1, REG1), (REG2, NEAR6), (FAR6,), (HALF,))


class Moves:
    def __init__(self, hidden, held, over, half_a, sends, recvs):
        r, p = lax.axis_index("region"), lax.axis_index("view")
        y, xh = r // 2, lax.rem(r, 2)
        z, col, core = p // 4, lax.rem(p // 2, 2), lax.rem(p, 2)
        f = 2 * col - 1
        self.sends, self.recvs, self.table = sends, recvs, {}

        def at(dz, column, c):
            return (r, lax.rem(z + dz + 8, 8) * 4 + column * 2 + c)

        other = 1 - col
        dy = 1 - 2 * xh
        self.cross = core != col
        self.has_to = (y + dy >= 0) & (y + dy <= 3)
        self.has_from = (y - dy >= 0) & (y - dy <= 3)
        sib, flip = at(0, col, 1 - core), at(0, other, core)
        xpair = (y * 2 + 1 - xh, z * 4 + other * 2 + core)
        y_to = (jnp.clip(y + dy, 0, 3) * 2 + xh, p)
        y_from = (jnp.clip(y - dy, 0, 3) * 2 + xh, p)
        step_to, step_from = at(-f, col, 1 - core), at(f, col, 1 - core)

        self.greet = [sib, flip, xpair, at(-f, col, core), at(2 * f, col, core), at(-2 * f, col, core), at(-2 * f, other, core)]
        self.greet_if = [(jnp.logical_not(self.cross), step_from), (self.has_from, y_from)]
        self.partners = 7 + self.cross.astype(jnp.int32) + self.has_to.astype(jnp.int32)

        place = lambda region, dev: region * 32 + dev[1]
        self.me = r * 32 + p
        nowhere = jnp.int32(-7)
        self.views = {
            SIB: place(r, sib),
            STEP1: jnp.where(self.cross, place(r, at(0, other, 1 - core)), place(r, at(f, other, 1 - core))),
            REG1: (y * 2 + 1 - xh) * 32 + p,
            REG2: jnp.where(self.has_from, ((y - dy) * 2 + 1 - xh) * 32 + p, nowhere),
            NEAR6: place(r, at(-f, other, core)),
            FAR6: place(r, at(2 * f, other, core)),
            HALF: place(r, at(4, col, core)),
        }

        slot = lambda i: held.at[pl.ds(i * TOK, TOK)]
        self.add("sib", hidden, slot(SIB), sib)
        for k, (first, size, kind) in enumerate(CHUNKS):
            cut = lambda ref: ref.at[:, pl.ds(first, size)]
            self.add(("flip", k), cut(hidden), cut(over), flip)
            if kind == "a":
                self.add(("two", k), cut(hidden), half_a, at(2 * f, col, core))
                self.add(("four", k), half_a, cut(slot(HALF)), at(2 * f, col, core))
                self.add(("side", k), half_a, cut(slot(FAR6)), flip)
            else:
                self.add(("two", k), cut(over), cut(slot(FAR6)), at(-2 * f, col, core))
                self.add(("four", k), cut(slot(FAR6)), cut(slot(HALF)), at(-2 * f, other, core))
            self.add(("near", k), cut(over), cut(slot(NEAR6)), at(f, col, core))
            self.add(("step", k), cut(over), cut(slot(STEP1)), sib, step_to)
            self.add(("xpair", k), cut(over), cut(slot(REG1)), xpair)
            self.add(("ypair", k), cut(slot(REG1)), cut(slot(REG2)), y_to)

    def add(self, key, src, dst, device, device_if_cross=None):
        i = len(self.table)
        make = lambda to: pltpu.make_async_remote_copy(
            src_ref=src, dst_ref=dst, send_sem=self.sends.at[i], recv_sem=self.recvs.at[i], device_id=to, device_id_type=MESH
        )
        self.table[key] = (make, device, device_if_cross)

    def start(self, key):
        make, device, device_if_cross = self.table[key]
        if device_if_cross is not None:
            @pl.when(self.cross)
            def _():
                make(device_if_cross).start()

            @pl.when(jnp.logical_not(self.cross))
            def _():
                make(device).start()
        elif key[0] == "ypair":
            @pl.when(self.has_to)
            def _():
                make(device).start()
        else:
            make(device).start()

    def arrived(self, key):
        make, device, _ = self.table[key]
        if key[0] == "ypair":
            @pl.when(self.has_from)
            def _():
                make(device).wait_recv()
        else:
            make(device).wait_recv()

    def sent(self, key):
        make, device, _ = self.table[key]
        if key[0] == "ypair":
            @pl.when(self.has_to)
            def _():
                make(device).wait_send()
        else:
            make(device).wait_send()

    def barrier(self):
        sem = pltpu.get_barrier_semaphore()
        tell = lambda dev: pl.semaphore_signal(sem, inc=1, device_id=dev, device_id_type=MESH)
        for dev in self.greet:
            tell(dev)
        for cond, dev in self.greet_if:
            @pl.when(cond)
            def _(dev=dev):
                tell(dev)
        return lambda: pl.semaphore_wait(sem, self.partners)


def project(rows, weight):
    return jnp.dot(rows, weight, preferred_element_type=F32)


def make_queries(x, wq, queries):
    q = project(x, wq[...])
    row = 0
    for tile, heads in WINDOWS:
        part = q[:, tile * 128 : tile * 128 + 256]
        lane = lax.broadcasted_iota(jnp.int32, (TOK, 256), 1) + tile * 128
        for h in heads:
            keep = (lane >= h * HEAD) & (lane < (h + 1) * HEAD)
            queries[row : row + TOK, :] = jnp.where(keep, part, 0.0).astype(BF)
            row += TOK


def attend(first, at, links, queries, keys, values_t, tops, totals, accum, scores, weights):
    m = len(links) * TOK
    row = 0
    for tile, heads in WINDOWS:
        n = len(heads) * TOK
        scores[:m, row : row + n] = lax.dot_general(
            keys[at : at + m, tile * 128 : tile * 128 + 256], queries[row : row + n, :], NT, preferred_element_type=F32
        )
        row += n
    shrink, newtops = [], []
    for h in range(HEADS):
        top = None
        for b, link in enumerate(links):
            x = jnp.max(scores[b * TOK : (b + 1) * TOK, h * TOK : (h + 1) * TOK], axis=0, keepdims=True)
            if link is not None:
                x = jnp.where(link, x, NEG)
            top = x if top is None else jnp.maximum(top, x)
        if not first:
            old = tops[h : h + 1, :]
            top = jnp.maximum(old, top)
            shrink.append(jnp.exp2((old - top) * SCALE2))
        newtops.append(top)
    for h in range(HEADS):
        total = None
        for b, link in enumerate(links):
            x = scores[b * TOK : (b + 1) * TOK, h * TOK : (h + 1) * TOK]
            top = newtops[h] if link is None else jnp.where(link, newtops[h], -NEG)
            w = jnp.exp2((x - top) * SCALE2)
            weights[b * TOK : (b + 1) * TOK, h * TOK : (h + 1) * TOK] = w.astype(BF)
            w = jnp.sum(w, axis=0, keepdims=True)
            total = w if total is None else total + w
        tops[h : h + 1, :] = newtops[h]
        totals[h : h + 1, :] = total if first else totals[h : h + 1, :] * shrink[h] + total
    for h in range(HEADS):
        start = HEAD * h - (8 if h % 2 else 0)
        o = jnp.dot(values_t[start : start + 80, at : at + m], weights[:m, h * TOK : (h + 1) * TOK], preferred_element_type=F32)
        o = o[8:80] if h % 2 else o[:72]
        accum[h] = o if first else accum[h] * shrink[h] + o


def finish(totals, accum, mixed_t, wo):
    for h in range(HEADS):
        mixed_t[h * HEAD : (h + 1) * HEAD, :] = accum[h] / totals[h : h + 1, :]
    mixed = jnp.concatenate([mixed_t[t * 128 : (t + 1) * 128, :].T.astype(BF) for t in range(D // 128)], axis=1)
    return project(mixed, wo[...]).astype(BF)


PROGRAM = (
    ("send", ("two", 0), ("flip", 1), ("flip", 0), "sib"),
    "links", "q", ("kv", (OWN,)),
    ("relay", ("flip", 1), ("two", 1), ("near", 1), ("step", 1), ("xpair", 1)),
    ("get", "sib"), ("kv", (SIB,)),
    ("relay", ("two", 0), ("four", 0), ("side", 0)),
    ("relay", ("flip", 0), ("near", 0), ("step", 0), ("xpair", 0)),
    ("attend", 0),
    ("relay", ("two", 1), ("four", 1)),
    ("relay", ("xpair", 1), ("ypair", 1)),
    ("relay", ("xpair", 0), ("ypair", 0)),
    ("get", ("step", 0), ("step", 1)), ("kv", (STEP1, REG1)), ("attend", 1),
    ("get", ("ypair", 0), ("ypair", 1), ("near", 0), ("near", 1)), ("kv", (REG2, NEAR6)), ("attend", 2),
    ("get", ("side", 0)), ("kv", (FAR6,)), ("attend", 3),
    ("get", ("four", 0), ("four", 1)), ("kv", (HALF,)), ("attend", 4),
    "finish",
)


def kernel(
    hidden, pairs, w_query, w_key, w_value, w_out, out,
    held, over, half_a, wq, wk, wv, wo, wvt, queries, keys, values_t, tops, totals, accum, scores, weights, mixed_t,
    sends, recvs, local,
):
    moves = Moves(hidden, held, over, half_a, sends, recvs)
    wait_barrier = moves.barrier()
    loads = {
        name: pltpu.make_async_copy(src, dst, local.at[i])
        for i, (name, src, dst) in enumerate(
            (("x", hidden, held.at[pl.ds(0, TOK)]), ("wq", w_query, wq), ("wk", w_key, wk), ("wv", w_value, wv), ("wo", w_out, wo))
        )
    }
    for load in loads.values():
        load.start()

    @pl.when(jnp.logical_not(moves.has_from))
    def _():
        held[REG2 * TOK : (REG2 + 1) * TOK, :] = jnp.zeros((TOK, D), BF)

    wait_barrier()
    links = {OWN: None}
    for step in PROGRAM:
        verb, args = (step, ()) if isinstance(step, str) else (step[0], step[1:])
        if verb == "send":
            for key in args:
                moves.start(key)
        elif verb == "relay":
            moves.arrived(args[0])
            for key in args[1:]:
                moves.start(key)
        elif verb == "get":
            for key in args:
                moves.arrived(key)
        elif verb == "links":
            low, high = pairs[0:1, :], pairs[1:2, :]
            for slot, view in moves.views.items():
                hit = ((low == moves.me) & (high == view)) | ((low == view) & (high == moves.me))
                any_hit = jnp.max(jnp.where(hit, 1.0, 0.0), axis=1, keepdims=True)
                links[slot] = jnp.broadcast_to(any_hit, (1, TOK)) > 0.5
        elif verb == "q":
            loads["x"].wait()
            loads["wq"].wait()
            make_queries(held[:TOK, :], wq, queries)
        elif verb == "kv":
            slots = args[0]
            if slots == (OWN,):
                loads["wk"].wait()
            rows = slice(slots[0] * TOK, (slots[-1] + 1) * TOK)
            keys[rows, :] = project(held[rows, :], wk[...]).astype(BF)
            if slots == (OWN,):
                loads["wv"].wait()
                for i in range(D // 128):
                    wvt[i * 128 : (i + 1) * 128, :] = wv[:, i * 128 : (i + 1) * 128].T
            values_t[:, rows] = lax.dot_general(wvt[...], held[rows, :], NT, preferred_element_type=F32).astype(BF)
        elif verb == "attend":
            slots = GROUPS[args[0]]
            attend(
                args[0] == 0, slots[0] * TOK, [links[s] for s in slots],
                queries, keys, values_t, tops, totals, accum, scores, weights,
            )
        elif verb == "finish":
            loads["wo"].wait()
            out[...] = finish(totals, accum, mixed_t, wo)
    for key in moves.table:
        moves.sent(key)


def per_device(hidden, pairs, w_query, w_key, w_value, w_out):
    any_space, vmem = pl.BlockSpec(memory_space=pl.ANY), pl.BlockSpec(memory_space=pltpu.VMEM)
    half = sum(size for _, size, kind in CHUNKS if kind == "a")
    bf = lambda *shape: pltpu.VMEM(shape, BF)
    f32 = lambda *shape: pltpu.VMEM(shape, F32)
    return pl.pallas_call(
        kernel,
        out_shape=jax.ShapeDtypeStruct((TOK, D), BF),
        in_specs=[any_space, vmem, any_space, any_space, any_space, any_space],
        out_specs=vmem,
        scratch_shapes=[
            bf(8 * TOK, D), bf(TOK, D), bf(TOK, half),
            bf(D, D), bf(D, D), bf(D, D), bf(D, D), bf(D, D),
            bf(HEADS * TOK, 256), bf(8 * TOK, D), bf(D, 8 * TOK),
            f32(HEADS, TOK), f32(HEADS, TOK), f32(HEADS, HEAD, TOK),
            f32(2 * TOK, HEADS * TOK), bf(2 * TOK, HEADS * TOK), f32(D, TOK),
            pltpu.SemaphoreType.DMA((32,)), pltpu.SemaphoreType.DMA((32,)), pltpu.SemaphoreType.DMA((5,)),
        ],
        compiler_params=pltpu.CompilerParams(collective_id=0, has_side_effects=True, vmem_limit_bytes=60 * 2**20),
        name="cross_view_attention",
    )(hidden, pairs.T, w_query, w_key, w_value, w_out)


def solution(mesh):
    in_specs = (P(("region", "view"), None), P(), P(), P(), P(), P())
    return jax.shard_map(
        per_device, mesh=mesh, in_specs=in_specs, out_specs=P(("region", "view"), None), check_vma=False
    )
```

```python
import functools

import jax
import jax.numpy as jnp
import numpy as np
from jax import lax
from jax.experimental import pallas as pl
from jax.experimental.pallas import tpu as pltpu
from jax.sharding import PartitionSpec as P

MESH = pl.DeviceIdType.MESH
BF, F32 = jnp.bfloat16, jnp.float32
D, TOK, HEADS, HEAD = 1152, 128, 16, 72
NEG = -1e30
SCALE2 = float(HEAD**-0.5 * np.log2(np.e))
NT = (((1,), (1,)), ((), ()))

WINDOWS = ((0, (0, 1, 2)), (1, (3, 4)), (2, (5, 6)), (3, (7,)), (4, (8, 9)), (5, (10, 11)), (6, (12, 13)), (7, (14, 15)))

OWN, SIB, REG1, FAR6, STEP1, NEAR6, REG2, HALF = range(8)

CHUNKS = ((0, 640, "a", "z"), (640, 512, "b", "x"))
GROUPS = ((OWN, SIB), (REG1, FAR6), (STEP1, NEAR6), (REG2,), (HALF,))


class Moves:
    def __init__(self, hidden, held, over, half_a, back, sends, recvs):
        r, p = lax.axis_index("region"), lax.axis_index("view")
        y, xh = r // 2, lax.rem(r, 2)
        z, col, core = p // 4, lax.rem(p // 2, 2), lax.rem(p, 2)
        f = 2 * col - 1
        self.sends, self.recvs, self.table = sends, recvs, {}

        def at(dz, column, c):
            return (r, lax.rem(z + dz + 8, 8) * 4 + column * 2 + c)

        other = 1 - col
        dy = 1 - 2 * xh
        self.cross = core != col
        self.has_to = (y + dy >= 0) & (y + dy <= 3)
        self.has_from = (y - dy >= 0) & (y - dy <= 3)
        sib, flip = at(0, col, 1 - core), at(0, other, core)
        xpair = (y * 2 + 1 - xh, z * 4 + other * 2 + core)
        y_to = (jnp.clip(y + dy, 0, 3) * 2 + xh, p)
        y_from = (jnp.clip(y - dy, 0, 3) * 2 + xh, p)
        step_to, step_from = at(-f, col, 1 - core), at(f, col, 1 - core)

        self.greet = [sib, flip, xpair, at(-f, col, core), at(f, col, core), at(2 * f, col, core), at(-2 * f, col, core), at(-2 * f, other, core)]
        self.greet_if = [(jnp.logical_not(self.cross), step_from), (self.has_from, y_from)]
        self.partners = 8 + self.cross.astype(jnp.int32) + self.has_to.astype(jnp.int32)

        place = lambda region, dev: region * 32 + dev[1]
        self.me = r * 32 + p
        nowhere = jnp.int32(-7)
        self.views = {
            SIB: place(r, sib),
            STEP1: jnp.where(self.cross, place(r, at(0, other, 1 - core)), place(r, at(f, other, 1 - core))),
            REG1: (y * 2 + 1 - xh) * 32 + p,
            REG2: jnp.where(self.has_from, ((y - dy) * 2 + 1 - xh) * 32 + p, nowhere),
            NEAR6: place(r, at(-f, other, core)),
            FAR6: place(r, at(2 * f, other, core)),
            HALF: place(r, at(4, col, core)),
        }

        slot = lambda i: held.at[pl.ds(i * TOK, TOK)]
        self.add("sib", hidden, slot(SIB), sib)
        for k, (first, size, kind, way) in enumerate(CHUNKS):
            cut = lambda ref: ref.at[:, pl.ds(first, size)]
            self.add(("flip", k), cut(hidden), cut(over), flip)
            if kind == "a":
                self.add(("two", k), cut(hidden), half_a, at(2 * f, col, core))
                self.add(("four", k), half_a, cut(slot(HALF)), at(2 * f, col, core))
                self.add(("side", k), half_a, cut(slot(FAR6)), flip)
            else:
                self.add(("two", k), cut(over), cut(slot(FAR6)), at(-2 * f, col, core))
                self.add(("four", k), cut(slot(FAR6)), cut(slot(HALF)), at(-2 * f, other, core))
            if way == "z":
                self.add(("back", k), cut(hidden), cut(back), at(-f, col, core))
                self.add(("near", k), cut(back), cut(slot(NEAR6)), flip)
            else:
                self.add(("near", k), cut(over), cut(slot(NEAR6)), at(f, col, core))
            self.add(("step", k), cut(over), cut(slot(STEP1)), sib, step_to)
            self.add(("xpair", k), cut(over), cut(slot(REG1)), xpair)
            self.add(("ypair", k), cut(slot(REG1)), cut(slot(REG2)), y_to)

    def add(self, key, src, dst, device, device_if_cross=None):
        i = len(self.table)
        make = lambda to: pltpu.make_async_remote_copy(
            src_ref=src, dst_ref=dst, send_sem=self.sends.at[i], recv_sem=self.recvs.at[i], device_id=to, device_id_type=MESH
        )
        self.table[key] = (make, device, device_if_cross)

    def start(self, key):
        make, device, device_if_cross = self.table[key]
        if device_if_cross is not None:
            @pl.when(self.cross)
            def _():
                make(device_if_cross).start()

            @pl.when(jnp.logical_not(self.cross))
            def _():
                make(device).start()
        elif key[0] == "ypair":
            @pl.when(self.has_to)
            def _():
                make(device).start()
        else:
            make(device).start()

    def arrived(self, key):
        make, device, _ = self.table[key]
        if key[0] == "ypair":
            @pl.when(self.has_from)
            def _():
                make(device).wait_recv()
        else:
            make(device).wait_recv()

    def sent(self, key):
        make, device, _ = self.table[key]
        if key[0] == "ypair":
            @pl.when(self.has_to)
            def _():
                make(device).wait_send()
        else:
            make(device).wait_send()

    def barrier(self):
        sem = pltpu.get_barrier_semaphore()
        tell = lambda dev: pl.semaphore_signal(sem, inc=1, device_id=dev, device_id_type=MESH)
        for dev in self.greet:
            tell(dev)
        for cond, dev in self.greet_if:
            @pl.when(cond)
            def _(dev=dev):
                tell(dev)
        return lambda: pl.semaphore_wait(sem, self.partners)


def project(rows, weight):
    return jnp.dot(rows, weight, preferred_element_type=F32)


def make_queries(x, wq, queries):
    q = project(x, wq[...])
    row = 0
    for tile, heads in WINDOWS:
        part = q[:, tile * 128 : tile * 128 + 256]
        lane = lax.broadcasted_iota(jnp.int32, (TOK, 256), 1) + tile * 128
        for h in heads:
            keep = (lane >= h * HEAD) & (lane < (h + 1) * HEAD)
            queries[row : row + TOK, :] = jnp.where(keep, part, 0.0).astype(BF)
            row += TOK


def attend(first, at, links, queries, keys, values_t, tops, totals, accum, scores, weights):
    m = len(links) * TOK
    row = 0
    for tile, heads in WINDOWS:
        n = len(heads) * TOK
        scores[:m, row : row + n] = lax.dot_general(
            keys[at : at + m, tile * 128 : tile * 128 + 256], queries[row : row + n, :], NT, preferred_element_type=F32
        )
        row += n
    shrink, newtops = [], []
    for h in range(HEADS):
        top = None
        for b, link in enumerate(links):
            x = jnp.max(scores[b * TOK : (b + 1) * TOK, h * TOK : (h + 1) * TOK], axis=0, keepdims=True)
            if link is not None:
                x = jnp.where(link, x, NEG)
            top = x if top is None else jnp.maximum(top, x)
        if not first:
            old = tops[h : h + 1, :]
            top = jnp.maximum(old, top)
            shrink.append(jnp.exp2((old - top) * SCALE2))
        newtops.append(top)
    for h in range(HEADS):
        total = None
        for b, link in enumerate(links):
            x = scores[b * TOK : (b + 1) * TOK, h * TOK : (h + 1) * TOK]
            top = newtops[h] if link is None else jnp.where(link, newtops[h], -NEG)
            w = jnp.exp2((x - top) * SCALE2)
            weights[b * TOK : (b + 1) * TOK, h * TOK : (h + 1) * TOK] = w.astype(BF)
            w = jnp.sum(w, axis=0, keepdims=True)
            total = w if total is None else total + w
        tops[h : h + 1, :] = newtops[h]
        totals[h : h + 1, :] = total if first else totals[h : h + 1, :] * shrink[h] + total
    for h in range(HEADS):
        start = HEAD * h - (8 if h % 2 else 0)
        o = jnp.dot(values_t[start : start + 80, at : at + m], weights[:m, h * TOK : (h + 1) * TOK], preferred_element_type=F32)
        o = o[8:80] if h % 2 else o[:72]
        accum[h] = o if first else accum[h] * shrink[h] + o


def finish(totals, accum, mixed_t, wo):
    for h in range(HEADS):
        mixed_t[h * HEAD : (h + 1) * HEAD, :] = accum[h] / totals[h : h + 1, :]
    mixed = jnp.concatenate([mixed_t[t * 128 : (t + 1) * 128, :].T.astype(BF) for t in range(D // 128)], axis=1)
    return project(mixed, wo[...]).astype(BF)


PROGRAM = (
    ("send", ("two", 0), ("flip", 1), ("flip", 0), ("back", 0), "sib"),
    "links", "q",
    ("key", (OWN,)), "turn",
    ("relay", ("flip", 1), ("two", 1), ("near", 1), ("step", 1), ("xpair", 1)),
    ("relay", ("back", 0), ("near", 0)),
    ("value", (OWN,)),
    ("get", "sib"), ("kv", (SIB,)), ("attend", 0),
    ("relay", ("two", 0), ("four", 0), ("side", 0)),
    ("relay", ("flip", 0), ("step", 0), ("xpair", 0)),
    ("relay", ("xpair", 1), ("ypair", 1)),
    ("relay", ("two", 1), ("four", 1)),
    ("relay", ("xpair", 0), ("ypair", 0)),
    ("get", ("side", 0)), ("kv", (REG1, FAR6)), ("attend", 1),
    ("get", ("step", 0), ("step", 1), ("near", 0), ("near", 1)), ("kv", (STEP1, NEAR6)), ("attend", 2),
    ("get", ("ypair", 0), ("ypair", 1)), ("kv", (REG2,)), ("attend", 3),
    ("get", ("four", 0), ("four", 1)), ("kv", (HALF,)), ("attend", 4),
    "finish",
)


def kernel(
    hidden, pairs, w_query, w_key, w_value, w_out, out,
    held, over, half_a, back, wq, wk, wv, wo, wvt, queries, keys, values_t, tops, totals, accum, scores, weights, mixed_t,
    sends, recvs, local,
):
    moves = Moves(hidden, held, over, half_a, back, sends, recvs)
    wait_barrier = moves.barrier()
    loads = {
        name: pltpu.make_async_copy(src, dst, local.at[i])
        for i, (name, src, dst) in enumerate(
            (("x", hidden, held.at[pl.ds(0, TOK)]), ("wq", w_query, wq), ("wk", w_key, wk), ("wv", w_value, wv), ("wo", w_out, wo))
        )
    }
    for load in loads.values():
        load.start()

    @pl.when(jnp.logical_not(moves.has_from))
    def _():
        held[REG2 * TOK : (REG2 + 1) * TOK, :] = jnp.zeros((TOK, D), BF)

    wait_barrier()
    links = {OWN: None}
    for step in PROGRAM:
        verb, args = (step, ()) if isinstance(step, str) else (step[0], step[1:])
        if verb == "send":
            for key in args:
                moves.start(key)
        elif verb == "relay":
            moves.arrived(args[0])
            for key in args[1:]:
                moves.start(key)
        elif verb == "get":
            for key in args:
                moves.arrived(key)
        elif verb == "links":
            low, high = pairs[0:1, :], pairs[1:2, :]
            for slot, view in moves.views.items():
                hit = ((low == moves.me) & (high == view)) | ((low == view) & (high == moves.me))
                any_hit = jnp.max(jnp.where(hit, 1.0, 0.0), axis=1, keepdims=True)
                links[slot] = jnp.broadcast_to(any_hit, (1, TOK)) > 0.5
        elif verb == "q":
            loads["x"].wait()
            loads["wq"].wait()
            make_queries(held[:TOK, :], wq, queries)
        elif verb == "turn":
            loads["wv"].wait()
            for i in range(D // 128):
                wvt[i * 128 : (i + 1) * 128, :] = wv[:, i * 128 : (i + 1) * 128].T
        elif verb in ("kv", "key", "value"):
            slots = args[0]
            rows = slice(slots[0] * TOK, (slots[-1] + 1) * TOK)
            if verb != "value":
                if OWN in slots:
                    loads["wk"].wait()
                keys[rows, :] = project(held[rows, :], wk[...]).astype(BF)
            if verb != "key":
                values_t[:, rows] = lax.dot_general(wvt[...], held[rows, :], NT, preferred_element_type=F32).astype(BF)
        elif verb == "attend":
            slots = GROUPS[args[0]]
            attend(
                args[0] == 0, slots[0] * TOK, [links[s] for s in slots],
                queries, keys, values_t, tops, totals, accum, scores, weights,
            )
        elif verb == "finish":
            loads["wo"].wait()
            out[...] = finish(totals, accum, mixed_t, wo)
    for key in moves.table:
        moves.sent(key)


def per_device(hidden, pairs, w_query, w_key, w_value, w_out):
    any_space, vmem = pl.BlockSpec(memory_space=pl.ANY), pl.BlockSpec(memory_space=pltpu.VMEM)
    half = sum(c[1] for c in CHUNKS if c[2] == "a")
    bf = lambda *shape: pltpu.VMEM(shape, BF)
    f32 = lambda *shape: pltpu.VMEM(shape, F32)
    return pl.pallas_call(
        kernel,
        out_shape=pltpu.VMEM((TOK, D), BF),
        in_specs=[any_space, vmem, any_space, any_space, any_space, any_space],
        out_specs=vmem,
        scratch_shapes=[
            bf(8 * TOK, D), bf(TOK, D), bf(TOK, half), bf(TOK, D),
            bf(D, D), bf(D, D), bf(D, D), bf(D, D), bf(D, D),
            bf(HEADS * TOK, 256), bf(8 * TOK, D), bf(D, 8 * TOK),
            f32(HEADS, TOK), f32(HEADS, TOK), f32(HEADS, HEAD, TOK),
            f32(2 * TOK, HEADS * TOK), bf(2 * TOK, HEADS * TOK), f32(D, TOK),
            pltpu.SemaphoreType.DMA((32,)), pltpu.SemaphoreType.DMA((32,)), pltpu.SemaphoreType.DMA((5,)),
        ],
        compiler_params=pltpu.CompilerParams(collective_id=0, has_side_effects=True, vmem_limit_bytes=60 * 2**20),
        name="cross_view_attention",
    )(hidden, pairs.T, w_query, w_key, w_value, w_out)


def solution(mesh):
    in_specs = (P(("region", "view"), None), P(), P(), P(), P(), P())
    return jax.shard_map(
        per_device, mesh=mesh, in_specs=in_specs, out_specs=P(("region", "view"), None), check_vma=False
    )
```

```python
import functools

import jax
import jax.numpy as jnp
import numpy as np
from jax import lax
from jax.experimental import pallas as pl
from jax.experimental.pallas import tpu as pltpu
from jax.sharding import PartitionSpec as P

MESH = pl.DeviceIdType.MESH
BF, F32 = jnp.bfloat16, jnp.float32
D, TOK, HEADS, HEAD = 1152, 128, 16, 72
NEG = -1e30
SCALE2 = float(HEAD**-0.5 * np.log2(np.e))
NT = (((1,), (1,)), ((), ()))

WINDOWS = ((0, (0, 1, 2)), (1, (3, 4)), (2, (5, 6)), (3, (7,)), (4, (8, 9)), (5, (10, 11)), (6, (12, 13)), (7, (14, 15)))

OWN, SIB, NEAR6, FAR6, STEP1, REG1, REG2, HALF = range(8)

CHUNKS = ((0, 640, "a", "z"), (640, 512, "b", "x"))
GROUPS = ((OWN, SIB), (NEAR6, FAR6), (STEP1, REG1), (REG2, HALF))


class Moves:
    def __init__(self, hidden, held, over, half_a, back, sends, recvs):
        r, p = lax.axis_index("region"), lax.axis_index("view")
        y, xh = r // 2, lax.rem(r, 2)
        z, col, core = p // 4, lax.rem(p // 2, 2), lax.rem(p, 2)
        f = 2 * col - 1
        self.sends, self.recvs, self.table = sends, recvs, {}

        def at(dz, column, c):
            return (r, lax.rem(z + dz + 8, 8) * 4 + column * 2 + c)

        other = 1 - col
        dy = 1 - 2 * xh
        self.cross = core != col
        self.has_y = (y - dy >= 0) & (y - dy <= 3)
        sib, flip = at(0, col, 1 - core), at(0, other, core)
        xpair = (y * 2 + 1 - xh, z * 4 + other * 2 + core)
        ypair = (jnp.clip(y - dy, 0, 3) * 2 + 1 - xh, z * 4 + other * 2 + core)
        step_to, step_from = at(-f, col, 1 - core), at(f, col, 1 - core)

        self.greet = [sib, flip, xpair, at(-f, col, core), at(f, col, core), at(2 * f, col, core), at(-2 * f, col, core), at(-2 * f, other, core)]
        self.greet_if = [(jnp.logical_not(self.cross), step_from), (self.has_y, ypair)]
        self.partners = 8 + self.cross.astype(jnp.int32) + self.has_y.astype(jnp.int32)

        place = lambda region, dev: region * 32 + dev[1]
        self.me = r * 32 + p
        nowhere = jnp.int32(-7)
        self.views = {
            SIB: place(r, sib),
            STEP1: jnp.where(self.cross, place(r, at(0, other, 1 - core)), place(r, at(f, other, 1 - core))),
            REG1: (y * 2 + 1 - xh) * 32 + p,
            REG2: jnp.where(self.has_y, ((y - dy) * 2 + 1 - xh) * 32 + p, nowhere),
            NEAR6: place(r, at(-f, other, core)),
            FAR6: place(r, at(2 * f, other, core)),
            HALF: place(r, at(4, col, core)),
        }

        slot = lambda i: held.at[pl.ds(i * TOK, TOK)]
        self.add("sib", hidden, slot(SIB), sib)
        for k, (first, size, kind, way) in enumerate(CHUNKS):
            cut = lambda ref: ref.at[:, pl.ds(first, size)]
            self.add(("flip", k), cut(hidden), cut(over), flip)
            if kind == "a":
                self.add(("two", k), cut(hidden), half_a, at(2 * f, col, core))
                self.add(("four", k), half_a, cut(slot(HALF)), at(2 * f, col, core))
                self.add(("side", k), half_a, cut(slot(FAR6)), flip)
            else:
                self.add(("two", k), cut(over), cut(slot(FAR6)), at(-2 * f, col, core))
                self.add(("four", k), cut(slot(FAR6)), cut(slot(HALF)), at(-2 * f, other, core))
            if way == "z":
                self.add(("back", k), cut(hidden), cut(back), at(-f, col, core))
                self.add(("near", k), cut(back), cut(slot(NEAR6)), flip)
            else:
                self.add(("near", k), cut(over), cut(slot(NEAR6)), at(f, col, core))
            self.add(("step", k), cut(over), cut(slot(STEP1)), sib, step_to)
            self.add(("xpair", k), cut(over), cut(slot(REG1)), xpair)
            self.add(("ypair", k), cut(over), cut(slot(REG2)), ypair)

    def add(self, key, src, dst, device, device_if_cross=None):
        i = len(self.table)
        make = lambda to: pltpu.make_async_remote_copy(
            src_ref=src, dst_ref=dst, send_sem=self.sends.at[i], recv_sem=self.recvs.at[i], device_id=to, device_id_type=MESH
        )
        self.table[key] = (make, device, device_if_cross)

    def start(self, key):
        make, device, device_if_cross = self.table[key]
        if device_if_cross is not None:
            @pl.when(self.cross)
            def _():
                make(device_if_cross).start()

            @pl.when(jnp.logical_not(self.cross))
            def _():
                make(device).start()
        elif key[0] == "ypair":
            @pl.when(self.has_y)
            def _():
                make(device).start()
        else:
            make(device).start()

    def arrived(self, key):
        make, device, _ = self.table[key]
        if key[0] == "ypair":
            @pl.when(self.has_y)
            def _():
                make(device).wait_recv()
        else:
            make(device).wait_recv()

    def sent(self, key):
        make, device, _ = self.table[key]
        if key[0] == "ypair":
            @pl.when(self.has_y)
            def _():
                make(device).wait_send()
        else:
            make(device).wait_send()

    def barrier(self):
        sem = pltpu.get_barrier_semaphore()
        tell = lambda dev: pl.semaphore_signal(sem, inc=1, device_id=dev, device_id_type=MESH)
        for dev in self.greet:
            tell(dev)
        for cond, dev in self.greet_if:
            @pl.when(cond)
            def _(dev=dev):
                tell(dev)
        return lambda: pl.semaphore_wait(sem, self.partners)


def project(rows, weight):
    return jnp.dot(rows, weight, preferred_element_type=F32)


def make_queries(x, wq, queries):
    q = project(x, wq[...])
    row = 0
    for tile, heads in WINDOWS:
        part = q[:, tile * 128 : tile * 128 + 256]
        lane = lax.broadcasted_iota(jnp.int32, (TOK, 256), 1) + tile * 128
        for h in heads:
            keep = (lane >= h * HEAD) & (lane < (h + 1) * HEAD)
            queries[row : row + TOK, :] = jnp.where(keep, part, 0.0).astype(BF)
            row += TOK


def attend(first, at, links, queries, keys, values_t, tops, totals, accum, scores, weights):
    m = len(links) * TOK
    row = 0
    for tile, heads in WINDOWS:
        n = len(heads) * TOK
        scores[:m, row : row + n] = lax.dot_general(
            keys[at : at + m, tile * 128 : tile * 128 + 256], queries[row : row + n, :], NT, preferred_element_type=F32
        )
        row += n
    shrink, newtops = [], []
    for h in range(HEADS):
        top = None
        for b, link in enumerate(links):
            x = jnp.max(scores[b * TOK : (b + 1) * TOK, h * TOK : (h + 1) * TOK], axis=0, keepdims=True)
            if link is not None:
                x = jnp.where(link, x, NEG)
            top = x if top is None else jnp.maximum(top, x)
        if not first:
            old = tops[h : h + 1, :]
            top = jnp.maximum(old, top)
            shrink.append(jnp.exp2((old - top) * SCALE2))
        newtops.append(top)
    for h in range(HEADS):
        total = None
        for b, link in enumerate(links):
            x = scores[b * TOK : (b + 1) * TOK, h * TOK : (h + 1) * TOK]
            top = newtops[h] if link is None else jnp.where(link, newtops[h], -NEG)
            w = jnp.exp2((x - top) * SCALE2)
            weights[b * TOK : (b + 1) * TOK, h * TOK : (h + 1) * TOK] = w.astype(BF)
            w = jnp.sum(w, axis=0, keepdims=True)
            total = w if total is None else total + w
        tops[h : h + 1, :] = newtops[h]
        totals[h : h + 1, :] = total if first else totals[h : h + 1, :] * shrink[h] + total
    for h in range(HEADS):
        start = HEAD * h - (8 if h % 2 else 0)
        o = jnp.dot(values_t[start : start + 80, at : at + m], weights[:m, h * TOK : (h + 1) * TOK], preferred_element_type=F32)
        o = o[8:80] if h % 2 else o[:72]
        accum[h] = o if first else accum[h] * shrink[h] + o


def finish(totals, accum, mixed_t, wo):
    for h in range(HEADS):
        mixed_t[h * HEAD : (h + 1) * HEAD, :] = accum[h] / totals[h : h + 1, :]
    mixed = jnp.concatenate([mixed_t[t * 128 : (t + 1) * 128, :].T.astype(BF) for t in range(D // 128)], axis=1)
    return project(mixed, wo[...]).astype(BF)


PROGRAM = (
    ("send", ("two", 0), ("flip", 1), ("flip", 0), ("back", 0), "sib"),
    "links", "q",
    ("key", (OWN,)), "turn",
    ("relay", ("flip", 1), ("two", 1), ("near", 1), ("step", 1), ("xpair", 1), ("ypair", 1)),
    ("relay", ("back", 0), ("near", 0)),
    ("value", (OWN,)),
    ("get", "sib"), ("kv", (SIB,)), ("attend", 0),
    ("relay", ("two", 0), ("four", 0), ("side", 0)),
    ("relay", ("flip", 0), ("ypair", 0), ("step", 0), ("xpair", 0)),
    ("get", ("near", 0), ("near", 1)), ("kv", (NEAR6,)),
    ("relay", ("two", 1), ("four", 1)),
    ("get", ("side", 0)), ("kv", (FAR6,)), ("attend", 1),
    ("get", ("step", 0), ("step", 1), ("xpair", 0), ("xpair", 1)), ("kv", (STEP1, REG1)), ("attend", 2),
    ("get", ("ypair", 0), ("ypair", 1)), ("kv", (REG2,)),
    ("get", ("four", 0), ("four", 1)), ("kv", (HALF,)), ("attend", 3),
    "finish",
)


def kernel(
    hidden, pairs, w_query, w_key, w_value, w_out, out,
    held, over, half_a, back, wq, wk, wv, wo, wvt, queries, keys, values_t, tops, totals, accum, scores, weights, mixed_t,
    sends, recvs, local,
):
    moves = Moves(hidden, held, over, half_a, back, sends, recvs)
    wait_barrier = moves.barrier()
    loads = {
        name: pltpu.make_async_copy(src, dst, local.at[i])
        for i, (name, src, dst) in enumerate(
            (("x", hidden, held.at[pl.ds(0, TOK)]), ("wq", w_query, wq), ("wk", w_key, wk), ("wv", w_value, wv), ("wo", w_out, wo))
        )
    }
    for load in loads.values():
        load.start()

    @pl.when(jnp.logical_not(moves.has_y))
    def _():
        held[REG2 * TOK : (REG2 + 1) * TOK, :] = jnp.zeros((TOK, D), BF)

    wait_barrier()
    links = {OWN: None}
    for step in PROGRAM:
        verb, args = (step, ()) if isinstance(step, str) else (step[0], step[1:])
        if verb == "send":
            for key in args:
                moves.start(key)
        elif verb == "relay":
            moves.arrived(args[0])
            for key in args[1:]:
                moves.start(key)
        elif verb == "get":
            for key in args:
                moves.arrived(key)
        elif verb == "links":
            low, high = pairs[0:1, :], pairs[1:2, :]
            for slot, view in moves.views.items():
                hit = ((low == moves.me) & (high == view)) | ((low == view) & (high == moves.me))
                any_hit = jnp.max(jnp.where(hit, 1.0, 0.0), axis=1, keepdims=True)
                links[slot] = jnp.broadcast_to(any_hit, (1, TOK)) > 0.5
        elif verb == "q":
            loads["x"].wait()
            loads["wq"].wait()
            make_queries(held[:TOK, :], wq, queries)
        elif verb == "turn":
            loads["wv"].wait()
            for i in range(D // 128):
                wvt[i * 128 : (i + 1) * 128, :] = wv[:, i * 128 : (i + 1) * 128].T
        elif verb in ("kv", "key", "value"):
            slots = args[0]
            rows = slice(slots[0] * TOK, (slots[-1] + 1) * TOK)
            if verb != "value":
                if OWN in slots:
                    loads["wk"].wait()
                keys[rows, :] = project(held[rows, :], wk[...]).astype(BF)
            if verb != "key":
                values_t[:, rows] = lax.dot_general(wvt[...], held[rows, :], NT, preferred_element_type=F32).astype(BF)
        elif verb == "attend":
            slots = GROUPS[args[0]]
            attend(
                args[0] == 0, slots[0] * TOK, [links[s] for s in slots],
                queries, keys, values_t, tops, totals, accum, scores, weights,
            )
        elif verb == "finish":
            loads["wo"].wait()
            out[...] = finish(totals, accum, mixed_t, wo)
    for key in moves.table:
        moves.sent(key)


def per_device(hidden, pairs, w_query, w_key, w_value, w_out):
    any_space, vmem = pl.BlockSpec(memory_space=pl.ANY), pl.BlockSpec(memory_space=pltpu.VMEM)
    half = sum(c[1] for c in CHUNKS if c[2] == "a")
    bf = lambda *shape: pltpu.VMEM(shape, BF)
    f32 = lambda *shape: pltpu.VMEM(shape, F32)
    return pl.pallas_call(
        kernel,
        out_shape=pltpu.VMEM((TOK, D), BF),
        in_specs=[any_space, vmem, any_space, any_space, any_space, any_space],
        out_specs=vmem,
        scratch_shapes=[
            bf(8 * TOK, D), bf(TOK, D), bf(TOK, half), bf(TOK, D),
            bf(D, D), bf(D, D), bf(D, D), bf(D, D), bf(D, D),
            bf(HEADS * TOK, 256), bf(8 * TOK, D), bf(D, 8 * TOK),
            f32(HEADS, TOK), f32(HEADS, TOK), f32(HEADS, HEAD, TOK),
            f32(2 * TOK, HEADS * TOK), bf(2 * TOK, HEADS * TOK), f32(D, TOK),
            pltpu.SemaphoreType.DMA((32,)), pltpu.SemaphoreType.DMA((32,)), pltpu.SemaphoreType.DMA((5,)),
        ],
        compiler_params=pltpu.CompilerParams(collective_id=0, has_side_effects=True, vmem_limit_bytes=60 * 2**20),
        name="cross_view_attention",
    )(hidden, pairs.T, w_query, w_key, w_value, w_out)


def solution(mesh):
    in_specs = (P(("region", "view"), None), P(), P(), P(), P(), P())
    return jax.shard_map(
        per_device, mesh=mesh, in_specs=in_specs, out_specs=P(("region", "view"), None), check_vma=False
    )
```

```python
import functools

import jax
import jax.numpy as jnp
import numpy as np
from jax import lax
from jax.experimental import pallas as pl
from jax.experimental.pallas import tpu as pltpu
from jax.sharding import PartitionSpec as P

MESH = pl.DeviceIdType.MESH
BF, F32 = jnp.bfloat16, jnp.float32
D, TOK, HEADS, HEAD = 1152, 128, 16, 72
NEG = -1e30
SCALE2 = float(HEAD**-0.5 * np.log2(np.e))
NT = (((1,), (1,)), ((), ()))

WINDOWS = ((0, (0, 1, 2)), (1, (3, 4)), (2, (5, 6)), (3, (7,)), (4, (8, 9)), (5, (10, 11)), (6, (12, 13)), (7, (14, 15)))

OWN, SIB, NEAR6, FAR6, STEP1, REG1, REG2, HALF = range(8)

CHUNKS = ((0, 640, "a", "z"), (640, 512, "b", "x"))
GROUPS = ((OWN, SIB), (NEAR6, FAR6), (STEP1, REG1), (REG2, HALF))


class Moves:
    def __init__(self, hidden, held, over, half_a, back, sends, recvs):
        r, p = lax.axis_index("region"), lax.axis_index("view")
        y, xh = r // 2, lax.rem(r, 2)
        z, col, core = p // 4, lax.rem(p // 2, 2), lax.rem(p, 2)
        f = 2 * col - 1
        self.sends, self.recvs, self.table = sends, recvs, {}

        def at(dz, column, c):
            return (r, lax.rem(z + dz + 8, 8) * 4 + column * 2 + c)

        other = 1 - col
        dy = 1 - 2 * xh
        self.cross = core != col
        self.has_y = (y - dy >= 0) & (y - dy <= 3)
        sib, flip = at(0, col, 1 - core), at(0, other, core)
        xpair = (y * 2 + 1 - xh, z * 4 + other * 2 + core)
        ypair = (jnp.clip(y - dy, 0, 3) * 2 + 1 - xh, z * 4 + other * 2 + core)
        step_to, step_from = at(-f, col, 1 - core), at(f, col, 1 - core)

        self.greet = [sib, flip, xpair, at(-f, col, core), at(f, col, core), at(2 * f, col, core), at(-2 * f, col, core), at(-2 * f, other, core)]
        self.greet_if = [(jnp.logical_not(self.cross), step_from), (self.has_y, ypair)]
        self.partners = 8 + self.cross.astype(jnp.int32) + self.has_y.astype(jnp.int32)

        place = lambda region, dev: region * 32 + dev[1]
        self.me = r * 32 + p
        nowhere = jnp.int32(-7)
        self.views = {
            SIB: place(r, sib),
            STEP1: jnp.where(self.cross, place(r, at(0, other, 1 - core)), place(r, at(f, other, 1 - core))),
            REG1: (y * 2 + 1 - xh) * 32 + p,
            REG2: jnp.where(self.has_y, ((y - dy) * 2 + 1 - xh) * 32 + p, nowhere),
            NEAR6: place(r, at(-f, other, core)),
            FAR6: place(r, at(2 * f, other, core)),
            HALF: place(r, at(4, col, core)),
        }

        slot = lambda i: held.at[pl.ds(i * TOK, TOK)]
        self.add("sib", hidden, slot(SIB), sib)
        for k, (first, size, kind, way) in enumerate(CHUNKS):
            cut = lambda ref: ref.at[:, pl.ds(first, size)]
            self.add(("flip", k), cut(hidden), cut(over), flip)
            if kind == "a":
                self.add(("two", k), cut(hidden), half_a, at(2 * f, col, core))
                self.add(("four", k), half_a, cut(slot(HALF)), at(2 * f, col, core))
                self.add(("side", k), half_a, cut(slot(FAR6)), flip)
            else:
                self.add(("two", k), cut(over), cut(slot(FAR6)), at(-2 * f, col, core))
                self.add(("four", k), cut(slot(FAR6)), cut(slot(HALF)), at(-2 * f, other, core))
            if way == "z":
                self.add(("back", k), cut(hidden), cut(back), at(-f, col, core))
                self.add(("near", k), cut(back), cut(slot(NEAR6)), flip)
            else:
                self.add(("near", k), cut(over), cut(slot(NEAR6)), at(f, col, core))
            self.add(("step", k), cut(over), cut(slot(STEP1)), sib, step_to)
            self.add(("xpair", k), cut(over), cut(slot(REG1)), xpair)
            self.add(("ypair", k), cut(over), cut(slot(REG2)), ypair)

    def add(self, key, src, dst, device, device_if_cross=None):
        i = len(self.table)
        make = lambda to: pltpu.make_async_remote_copy(
            src_ref=src, dst_ref=dst, send_sem=self.sends.at[i], recv_sem=self.recvs.at[i], device_id=to, device_id_type=MESH
        )
        self.table[key] = (make, device, device_if_cross)

    def start(self, key):
        make, device, device_if_cross = self.table[key]
        if device_if_cross is not None:
            @pl.when(self.cross)
            def _():
                make(device_if_cross).start()

            @pl.when(jnp.logical_not(self.cross))
            def _():
                make(device).start()
        elif key[0] == "ypair":
            @pl.when(self.has_y)
            def _():
                make(device).start()
        else:
            make(device).start()

    def arrived(self, key):
        make, device, _ = self.table[key]
        if key[0] == "ypair":
            @pl.when(self.has_y)
            def _():
                make(device).wait_recv()
        else:
            make(device).wait_recv()

    def sent(self, key):
        make, device, _ = self.table[key]
        if key[0] == "ypair":
            @pl.when(self.has_y)
            def _():
                make(device).wait_send()
        else:
            make(device).wait_send()

    def barrier(self):
        sem = pltpu.get_barrier_semaphore()
        tell = lambda dev: pl.semaphore_signal(sem, inc=1, device_id=dev, device_id_type=MESH)
        for dev in self.greet:
            tell(dev)
        for cond, dev in self.greet_if:
            @pl.when(cond)
            def _(dev=dev):
                tell(dev)
        return lambda: pl.semaphore_wait(sem, self.partners)


def project(rows, weight):
    return jnp.dot(rows, weight, preferred_element_type=F32)


def make_queries(x, wq, queries):
    q = project(x, wq[...])
    row = 0
    for tile, heads in WINDOWS:
        part = q[:, tile * 128 : tile * 128 + 256]
        lane = lax.broadcasted_iota(jnp.int32, (TOK, 256), 1) + tile * 128
        for h in heads:
            keep = (lane >= h * HEAD) & (lane < (h + 1) * HEAD)
            queries[row : row + TOK, :] = jnp.where(keep, part, 0.0).astype(BF)
            row += TOK


def attend(first, at, links, queries, keys, values_t, tops, totals, accum, scores, weights):
    m = len(links) * TOK
    row = 0
    for tile, heads in WINDOWS:
        n = len(heads) * TOK
        scores[:m, row : row + n] = lax.dot_general(
            keys[at : at + m, tile * 128 : tile * 128 + 256], queries[row : row + n, :], NT, preferred_element_type=F32
        )
        row += n
    shrink, newtops = [], []
    for h in range(HEADS):
        top = None
        for b, link in enumerate(links):
            x = jnp.max(scores[b * TOK : (b + 1) * TOK, h * TOK : (h + 1) * TOK], axis=0, keepdims=True)
            if link is not None:
                x = jnp.where(link, x, NEG)
            top = x if top is None else jnp.maximum(top, x)
        if not first:
            old = tops[h : h + 1, :]
            top = jnp.maximum(old, top)
            shrink.append(jnp.exp2((old - top) * SCALE2))
        newtops.append(top)
    for h in range(HEADS):
        total = None
        for b, link in enumerate(links):
            x = scores[b * TOK : (b + 1) * TOK, h * TOK : (h + 1) * TOK]
            top = newtops[h] if link is None else jnp.where(link, newtops[h], -NEG)
            w = jnp.exp2((x - top) * SCALE2)
            weights[b * TOK : (b + 1) * TOK, h * TOK : (h + 1) * TOK] = w.astype(BF)
            w = jnp.sum(w, axis=0, keepdims=True)
            total = w if total is None else total + w
        tops[h : h + 1, :] = newtops[h]
        totals[h : h + 1, :] = total if first else totals[h : h + 1, :] * shrink[h] + total
    for h in range(HEADS):
        start = HEAD * h - (8 if h % 2 else 0)
        o = jnp.dot(values_t[start : start + 80, at : at + m], weights[:m, h * TOK : (h + 1) * TOK], preferred_element_type=F32)
        o = o[8:80] if h % 2 else o[:72]
        accum[h] = o if first else accum[h] * shrink[h] + o


def finish(totals, accum, mixed_t, wo):
    for h in range(HEADS):
        mixed_t[h * HEAD : (h + 1) * HEAD, :] = accum[h] * (1.0 / totals[h : h + 1, :])
    mixed = jnp.concatenate([mixed_t[t * 128 : (t + 1) * 128, :].astype(BF).T for t in range(D // 128)], axis=1)
    return project(mixed, wo[...]).astype(BF)


PROGRAM = (
    ("send", ("two", 0), ("flip", 1), ("flip", 0), ("back", 0), "sib"),
    "links", "q",
    ("key", (OWN,)), "turn",
    ("relay", ("flip", 1), ("two", 1), ("near", 1), ("step", 1), ("xpair", 1), ("ypair", 1)),
    ("relay", ("back", 0), ("near", 0)),
    ("value", (OWN,)),
    ("get", "sib"), ("kv", (SIB,)), ("attend", 0),
    ("relay", ("two", 0), ("four", 0), ("side", 0)),
    ("relay", ("flip", 0), ("ypair", 0), ("step", 0), ("xpair", 0)),
    ("get", ("near", 0), ("near", 1)), ("kv", (NEAR6,)),
    ("relay", ("two", 1), ("four", 1)),
    ("get", ("side", 0)), ("kv", (FAR6,)), ("attend", 1),
    ("get", ("step", 0), ("step", 1), ("xpair", 0), ("xpair", 1)), ("kv", (STEP1, REG1)), ("attend", 2),
    ("get", ("ypair", 0), ("ypair", 1)), ("kv", (REG2,)),
    "wo", ("get", ("four", 0), ("four", 1)), ("kv", (HALF,)), ("attend", 3),
    "finish",
)


def kernel(
    hidden, pairs, w_query, w_key, w_value, w_out, out,
    held, over, half_a, back, wq, wk, wv, wo, wvt, queries, keys, values_t, tops, totals, accum, scores, weights, mixed_t,
    sends, recvs, local,
):
    moves = Moves(hidden, held, over, half_a, back, sends, recvs)
    wait_barrier = moves.barrier()
    loads = {
        name: pltpu.make_async_copy(src, dst, local.at[i])
        for i, (name, src, dst) in enumerate(
            (("x", hidden, held.at[pl.ds(0, TOK)]), ("wq", w_query, wq), ("wk", w_key, wk), ("wv", w_value, wv), ("wo", w_out, wo))
        )
    }
    for load in loads.values():
        load.start()

    @pl.when(jnp.logical_not(moves.has_y))
    def _():
        held[REG2 * TOK : (REG2 + 1) * TOK, :] = jnp.zeros((TOK, D), BF)

    wait_barrier()
    links = {OWN: None}
    for step in PROGRAM:
        verb, args = (step, ()) if isinstance(step, str) else (step[0], step[1:])
        if verb == "send":
            for key in args:
                moves.start(key)
        elif verb == "relay":
            moves.arrived(args[0])
            for key in args[1:]:
                moves.start(key)
        elif verb == "get":
            for key in args:
                moves.arrived(key)
        elif verb == "links":
            low, high = pairs[0:1, :], pairs[1:2, :]
            for slot, view in moves.views.items():
                hit = ((low == moves.me) & (high == view)) | ((low == view) & (high == moves.me))
                any_hit = jnp.max(jnp.where(hit, 1.0, 0.0), axis=1, keepdims=True)
                links[slot] = jnp.broadcast_to(any_hit, (1, TOK)) > 0.5
        elif verb == "q":
            loads["x"].wait()
            loads["wq"].wait()
            make_queries(held[:TOK, :], wq, queries)
        elif verb == "turn":
            loads["wv"].wait()
            for i in range(D // 128):
                wvt[i * 128 : (i + 1) * 128, :] = wv[:, i * 128 : (i + 1) * 128].T
        elif verb in ("kv", "key", "value"):
            slots = args[0]
            rows = slice(slots[0] * TOK, (slots[-1] + 1) * TOK)
            if verb != "value":
                if OWN in slots:
                    loads["wk"].wait()
                keys[rows, :] = project(held[rows, :], wk[...]).astype(BF)
            if verb != "key":
                values_t[:, rows] = lax.dot_general(wvt[...], held[rows, :], NT, preferred_element_type=F32).astype(BF)
        elif verb == "attend":
            slots = GROUPS[args[0]]
            attend(
                args[0] == 0, slots[0] * TOK, [links[s] for s in slots],
                queries, keys, values_t, tops, totals, accum, scores, weights,
            )
        elif verb == "wo":
            loads["wo"].wait()
        elif verb == "finish":
            out[...] = finish(totals, accum, mixed_t, wo)
    for key in moves.table:
        moves.sent(key)


def per_device(hidden, pairs, w_query, w_key, w_value, w_out):
    any_space, vmem = pl.BlockSpec(memory_space=pl.ANY), pl.BlockSpec(memory_space=pltpu.VMEM)
    half = sum(c[1] for c in CHUNKS if c[2] == "a")
    bf = lambda *shape: pltpu.VMEM(shape, BF)
    f32 = lambda *shape: pltpu.VMEM(shape, F32)
    return pl.pallas_call(
        kernel,
        out_shape=pltpu.VMEM((TOK, D), BF),
        in_specs=[any_space, vmem, any_space, any_space, any_space, any_space],
        out_specs=vmem,
        scratch_shapes=[
            bf(8 * TOK, D), bf(TOK, D), bf(TOK, half), bf(TOK, D),
            bf(D, D), bf(D, D), bf(D, D), bf(D, D), bf(D, D),
            bf(HEADS * TOK, 256), bf(8 * TOK, D), bf(D, 8 * TOK),
            f32(HEADS, TOK), f32(HEADS, TOK), f32(HEADS, HEAD, TOK),
            f32(2 * TOK, HEADS * TOK), bf(2 * TOK, HEADS * TOK), f32(D, TOK),
            pltpu.SemaphoreType.DMA((32,)), pltpu.SemaphoreType.DMA((32,)), pltpu.SemaphoreType.DMA((5,)),
        ],
        compiler_params=pltpu.CompilerParams(collective_id=0, has_side_effects=True, vmem_limit_bytes=60 * 2**20),
        name="cross_view_attention",
    )(hidden, pairs.T, w_query, w_key, w_value, w_out)


def solution(mesh):
    in_specs = (P(("region", "view"), None), P(), P(), P(), P(), P())
    return jax.shard_map(
        per_device, mesh=mesh, in_specs=in_specs, out_specs=P(("region", "view"), None), check_vma=False
    )
```
